256 devices in a mesh: node: 32 (over y, z), local: 8 (over x, core).
Axes of the slice: x: 4, y: 4, z: 8, core: 2. Of those that a mesh axis runs over, the one named last changes fastest.
Arguments:
- tokens: bfloat16 [4096, 7168], P('node', 'local'), may hold values from -6 to 6
- routes: int32 [4096, 8], P('node'), may hold values from 0 to 63, as said below
- gates: bfloat16 [4096, 8], P('node'), may hold values from 0.099609375 to 0.69921875
- w_gate: bfloat16 [256, 7168, 256], P(('node', 'local')), may hold values from -0.0625 to 0.0625
- w_up: bfloat16 [256, 7168, 256], P(('node', 'local')), may hold values from -0.0625 to 0.0625
- w_down: bfloat16 [256, 256, 7168], P(('node', 'local')), may hold values from -0.1875 to 0.1875
Outputs:
- mixed: bfloat16 [4096, 7168], P('node', 'local')
The draws below stay inside these ranges and needn't reach their ends.
Inputs may be any that keep to these rules, and one draw needn't show every extreme that they name: `routes`: each token names 8 different experts: all 2 experts of each of 4 different nodes, the node of expert e being e // 2, in any order. In each aligned block of 128 tokens no node is named by more than 24 tokens, and one node is named by exactly 24 tokens of every block.
All inputs are finite; a program needn't handle non-finite values.
Results may differ from the reference program's by a relative error of at most 0.02.
Values may be sent and summed in bfloat16 or wider, within the bound.
A program may use at most 128 MiB of HBM per device.

```python
import jax
import jax.numpy as jnp
from jax import lax

D = 7168
EXP_WIDTH = 1024
EXP_NODE = 2
NODE_LIMIT = 4
TOPK = 8
TOK_NODE = 128
TOKENS = 4096
EXPERTS = 64
EXP_SPLIT = 4
W_DEV = 256
CAP = 24
N_NODE = 32
N_LOCAL = 8


def draw_routes(key, part):
    key = jax.random.fold_in(key, 7)
    hot_key, weight_key, unit_key, order_key, column_key = jax.random.split(key, 5)
    blocks = N_NODE
    capacity = 6 * TOK_NODE // N_NODE
    units = NODE_LIMIT * TOK_NODE
    hottest = jax.random.randint(hot_key, (), 0, N_NODE)
    node_ids = jnp.arange(N_NODE, dtype=jnp.int32)
    node_weights = jax.random.randint(weight_key, (N_NODE,), 1, 5)
    start_counts = jnp.broadcast_to(jnp.where(node_ids == hottest, capacity, 0), (blocks, N_NODE)).astype(jnp.int32)

    def assign(unit_no, counts_now):
        scores = jax.random.randint(jax.random.fold_in(unit_key, unit_no), (blocks, N_NODE), 0, 1 << 16)
        ranked = scores * node_weights[None, :] * N_NODE + node_ids[None, :]
        ranked = jnp.where(counts_now < capacity, ranked, -1)
        chosen = lax.top_k(ranked, 1)[1][:, 0]
        return counts_now + (node_ids[None, :] == chosen[:, None]).astype(jnp.int32)
    counts = lax.fori_loop(0, units - capacity, assign, start_counts)
    ends = jnp.cumsum(counts, axis=1)
    positions = jnp.arange(units, dtype=jnp.int32)
    owner = jnp.sum((positions[None, :, None] >= ends[:, None, :]).astype(jnp.int32), axis=2)
    chosen_nodes = owner.reshape(blocks, NODE_LIMIT, TOK_NODE).transpose(0, 2, 1)
    token_scores = jax.random.randint(order_key, (blocks, TOK_NODE), 0, 1 << 20) * TOK_NODE + jnp.arange(TOK_NODE, dtype=jnp.int32)[None, :]
    token_order = jnp.argsort(token_scores, axis=1, stable=True)
    chosen_nodes = jnp.take_along_axis(chosen_nodes, token_order[:, :, None], axis=1)
    experts = chosen_nodes[:, :, :, None] * EXP_NODE + jnp.arange(EXP_NODE, dtype=jnp.int32)[None, None, None, :]
    experts = experts.reshape(blocks, TOK_NODE, TOPK)
    column_scores = jax.random.randint(column_key, (blocks, TOK_NODE, TOPK), 0, 1 << 20) * TOPK + jnp.arange(TOPK, dtype=jnp.int32)[None, None, :]
    column_order = jnp.argsort(column_scores, axis=2, stable=True)
    experts = jnp.take_along_axis(experts, column_order, axis=2)
    return experts.reshape(TOKENS, TOPK).astype(jnp.int32)


def block_scale(key, dims, shards, low, high):
    level = 1.0
    for dim, parts in shards:
        heights = jax.random.uniform(jax.random.fold_in(jax.random.fold_in(key, 6), dim), (parts,), jnp.float32, low / len(shards), high / len(shards))
        level = level * jnp.repeat(jnp.exp(heights), dims[dim] // parts).reshape((-1,) + (1,) * (len(dims) - 1 - dim))
    return level


def scatter_about(key, dims, deviation, reach, cuts=(), kind=jnp.bfloat16):
    level = block_scale(key, dims, cuts, -0.22, 0.18) if cuts else 1.0
    entries = jax.random.normal(key, dims, jnp.float32) * deviation * level
    return jnp.minimum(jnp.maximum(entries, -reach), reach).astype(kind)


def setup_inputs(seed: int = 0) -> dict:
    splits = jax.random.split(jax.random.key(seed), 7)
    return {
        "tokens": scatter_about(splits[0], (TOKENS, D), 1.0, 6.0, ((0, 32), (1, 8))),
        "routes": draw_routes(jax.random.fold_in(splits[6], 71), 0),
        "gates": jnp.clip(0.099609375 + 0.5996094 * jax.random.uniform(splits[2], (TOKENS, TOPK), jnp.float32) ** block_scale(splits[2], (TOKENS, TOPK), ((0, 32),), -0.2, 0.2), 0.099609375, 0.69921875).astype(jnp.bfloat16),
        "w_gate": scatter_about(splits[3], (EXPERTS * EXP_SPLIT, D, W_DEV), D ** -0.5, 0.0625, ((0, 256),)),
        "w_up": scatter_about(splits[4], (EXPERTS * EXP_SPLIT, D, W_DEV), D ** -0.5, 0.0625, ((0, 256),)),
        "w_down": scatter_about(splits[5], (EXPERTS * EXP_SPLIT, W_DEV, D), EXP_WIDTH ** -0.5, 0.1875, ((0, 256),)),
    }


def reference(tokens, routes, gates, w_gate, w_up, w_down):
    experts_all = EXP_NODE * N_NODE
    split_count = N_LOCAL // EXP_NODE
    slot_count = N_NODE * CAP
    expert_ids = jnp.arange(experts_all, dtype=jnp.int32)
    matches = routes[:, :, None] == expert_ids[None, None, :]
    weight = jnp.sum(jnp.where(matches, gates[:, :, None].astype(jnp.float32), jnp.float32(0.0)), axis=1)
    hit_counts = jnp.sum(matches.astype(jnp.int32), axis=1)
    node_hits = jnp.sum(hit_counts.reshape(TOKENS, N_NODE, EXP_NODE), axis=2)

    def node_step(summed_out, node_index):
        column = lax.dynamic_index_in_dim(node_hits, node_index, 1, keepdims=False)
        named = (column > 0).astype(jnp.int32)
        row_ids = jnp.nonzero(named > 0, size=slot_count, fill_value=0)[0].astype(jnp.int32)
        live_rows = (jnp.arange(slot_count, dtype=jnp.int32) < jnp.sum(named)).astype(jnp.float32)
        picked = tokens[row_ids]
        summed = jnp.zeros((slot_count, D), jnp.float32)
        for expert_no in range(EXP_NODE):
            expert = node_index * EXP_NODE + expert_no
            route_weight = weight[row_ids, expert][:, None]
            for slab_no in range(split_count):
                slab_index = expert * split_count + slab_no
                gate_act = jnp.dot(picked, w_gate[slab_index], preferred_element_type=jnp.float32)
                up_act = jnp.dot(picked, w_up[slab_index], preferred_element_type=jnp.float32)
                hidden = (jax.nn.silu(gate_act) * up_act * route_weight).astype(jnp.bfloat16)
                partial_value = jnp.dot(hidden, w_down[slab_index], preferred_element_type=jnp.float32).astype(jnp.bfloat16)
                partial_value = lax.optimization_barrier(partial_value)
                summed = summed + partial_value.astype(jnp.float32)
        node_out = lax.optimization_barrier(summed.astype(jnp.bfloat16))
        contribution = node_out.astype(jnp.float32) * live_rows[:, None]
        return summed_out.at[row_ids].add(contribution), None

    start_out = jnp.zeros((TOKENS, D), jnp.float32)
    final_out, unused = lax.scan(node_step, start_out, jnp.arange(N_NODE, dtype=jnp.int32))
    return final_out.astype(jnp.bfloat16)
```

```python
import jax
import jax.numpy as jnp
from jax import lax
from jax.experimental import pallas as pl
from jax.experimental.pallas import tpu as pltpu
from jax.sharding import PartitionSpec as P

F32, BF16 = jnp.float32, jnp.bfloat16
NY, NZ, NX = 4, 8, 4
TOK = 128
FEAT = 896
WIDTH = 256
DEPTH = FEAT * 8
CAP = 24
PAIR = 2 * CAP
ROWS = NY * PAIR
EARLY = 0
MAIN = FEAT - EARLY
WIDE = MAIN + 4 * EARLY
GATE = 128
CHUNKS = ((0, 4), (3, 5), (2, 6), (1, 7))
SLOT = {0: 0, 4: 1, 3: 2, 5: 3, 2: 4, 6: 5, 1: 6, 7: 7}
OWN = GATE
SIB = GATE + WIDE
SIDE = GATE + 2 * WIDE
MISSING = -100.0


def kernel(
    tok, routes_t, gates_t, wg_h, wu_h, wd_h, out,
    zb, meta_out, meta_in, onehot, picked, rows, wg, wu, wd, hid, osend, ret, zso, zsi, own,
    send_sem, recv_sem, local_sem,
):
    node, local = lax.axis_index("node"), lax.axis_index("local")
    y, z, x, c = node // NZ, node % NZ, local // 2, local % 2

    def dev(dx=0, dc=0, dy=0, dz=0):
        yy, zz = (y + dy + NY) % NY, (z + dz + NZ) % NZ
        xx, cc = (x + dx + NX) % NX, (c + dc) % 2
        return (yy * NZ + zz, xx * 2 + cc)

    counts = {"remote": 0, "local": 0}
    remote_copies = []

    def remote(src, dst, device):
        i = counts["remote"]
        counts["remote"] += 1
        copy = pltpu.make_async_remote_copy(
            src_ref=src, dst_ref=dst, send_sem=send_sem.at[i], recv_sem=recv_sem.at[i],
            device_id=device, device_id_type=pl.DeviceIdType.MESH,
        )
        copy.start()
        remote_copies.append(copy)
        return copy

    def load(src, dst):
        i = counts["local"]
        counts["local"] += 1
        copy = pltpu.make_async_copy(src, dst, local_sem.at[i])
        copy.start()
        return copy

    toward = 1 - 2 * c

    own_tokens = load(tok, zb.at[pl.ds(0, TOK), pl.ds(0, FEAT)])
    peers = (
        [dev(dx=i, dc=j) for i in range(NX) for j in range(2) if (i, j) != (0, 0)]
        + [dev(dy=i) for i in range(1, NY)]
        + [dev(dz=i) for i in range(1, NZ)]
    )
    barrier = pltpu.get_barrier_semaphore()
    for peer in peers:
        pl.semaphore_signal(barrier, inc=1, device_id=peer, device_id_type=pl.DeviceIdType.MESH)

    lane = lax.broadcasted_iota(jnp.int32, (TOK, TOK), 1)
    line = lax.broadcasted_iota(jnp.int32, (TOK, TOK), 0)
    step, kind = line // 16, line % 16
    target = ((y + kind % NY) % NY) * NZ + (z + step) % NZ
    expert = target * 2 + x // 2
    named = jnp.zeros((TOK, TOK), F32)
    weight = jnp.zeros((TOK, TOK), F32)
    routes_v, gates_v = routes_t[...], gates_t[...].astype(F32)
    for k in range(8):
        chosen = routes_v[k : k + 1, :]
        named = jnp.where(chosen // 2 == target, 1.0, named)
        weight = weight + jnp.where(chosen == expert, gates_v[k : k + 1, :], 0.0)
    before = jnp.where(line < lane, 1.0, 0.0).astype(BF16)
    earlier = jnp.dot(named.astype(BF16), before, preferred_element_type=F32)
    slots = jnp.where(named > 0.0, earlier, MISSING)
    meta = jnp.where(kind < 4, slots, jnp.where(kind < 8, weight, 0.0)).astype(BF16)
    meta_out[...] = meta
    meta_in[pl.ds(0, 16), :] = meta[0:16]

    own_tokens.wait()
    pl.semaphore_wait(barrier, len(peers))

    def block(i):
        return zb.at[pl.ds(SLOT[i] * TOK, TOK), :]

    if EARLY:
        first = [
            remote(
                zb.at[pl.ds(0, TOK), pl.ds(MAIN, EARLY)],
                zb.at[pl.ds(0, TOK), pl.ds(FEAT + j * EARLY, EARLY)],
                dev(dx=dx),
            )
            for j, dx in enumerate((1, -1, 2))
        ]
        for copy in first:
            copy.wait_recv()
    arrive = {1: remote(block(0), block(1), dev(dz=1)), 7: remote(block(0), block(7), dev(dz=-1))}
    metas = {
        i: remote(
            meta_out.at[pl.ds(16 * i, 16), :], meta_in.at[pl.ds(16 * SLOT[i], 16), :], dev(dz=i)
        )
        for i in range(1, NZ)
    }

    def first_row(dx, dc):
        return (((x + dx + NX) % NX) * 2 + (c + dc) % 2) * FEAT

    def aligned(i):
        return pl.multiple_of(i, 128)

    pieces = []
    for dc in range(2):
        pieces.append((first_row(0, dc), dc * WIDE, FEAT))
        if EARLY:
            for j, dx in enumerate((-1, 1, 2)):
                pieces.append((first_row(dx, dc) + MAIN, dc * WIDE + FEAT + j * EARLY, EARLY))
    for j, dx in enumerate((-1, 1, 2)):
        for dc in range(2):
            pieces.append((first_row(dx, dc), 2 * WIDE + (2 * j + dc) * MAIN, MAIN))
    weight_loads = []
    for src, dst, size in pieces:
        for hbm, vmem in ((wg_h, wg), (wu_h, wu)):
            weight_loads.append(
                load(hbm.at[0, pl.ds(aligned(src), size), :], vmem.at[pl.ds(dst, size), :])
            )
    down_load = load(wd_h.at[0, :, pl.ds(aligned(first_row(0, 0)), FEAT)], wd.at[pl.ds(0, WIDTH), :])
    downs = []
    for dx, dc, place in ((0, 1, 1), (1, 0, 2), (1, 1, 3), (-1, 0, 4), (-1, 1, 5), (2, 0, 6), (2, 1, 7)):
        downs.append(
            remote(
                wd_h.at[0, :, pl.ds(aligned(first_row(dx, dc)), FEAT)],
                wd.at[pl.ds(place * WIDTH, WIDTH), :],
                dev(dx=dx, dc=dc),
            )
        )

    for i in (1, 2):
        arrive[i].wait_recv()
        arrive[i + 1] = remote(block(i), block(i + 1), dev(dz=1))
        arrive[8 - i].wait_recv()
        arrive[7 - i] = remote(block(8 - i), block(7 - i), dev(dz=-1))
    arrive[3].wait_recv()
    arrive[5].wait_recv()
    arrive[4] = remote(zb.at[pl.ds((SLOT[3] + c) * TOK, TOK), :], block(4), dev(dz=toward))
    for copy in metas.values():
        copy.wait_recv()

    to_node, row_copies, sib_copies = {}, {}, {}
    hid_copies, hid_sibs, to_home, z_copies = {}, {}, {}, {}

    def select(k):
        near, far = (meta_in[pl.ds(16 * (2 * k + i), 16), :].astype(F32) for i in range(2))
        place = lax.broadcasted_iota(jnp.int32, (PAIR, 2 * TOK), 0).astype(F32)
        for j in range(NY):
            slot = jnp.concatenate([near[j : j + 1], far[j : j + 1] + CAP], axis=1)
            gate = jnp.concatenate([near[4 + j : 5 + j], far[4 + j : 5 + j]], axis=1)
            hit = jnp.where(place == slot, 1.0, 0.0)
            onehot[k, pl.ds(j * PAIR, PAIR), :] = hit.astype(BF16)
            share = jnp.sum(hit * gate, axis=1, keepdims=True)
            picked[k, pl.ds(j * PAIR, PAIR), pl.ds(0, GATE)] = jnp.broadcast_to(
                share, (PAIR, GATE)
            ).astype(BF16)
        chosen = jnp.dot(
            onehot[k], zb[pl.ds(2 * k * TOK, 2 * TOK), :], preferred_element_type=F32
        ).astype(BF16)
        picked[k, :, pl.ds(GATE, WIDE)] = chosen
        to_node[k] = [
            remote(
                picked.at[k, pl.ds(j * PAIR, PAIR), :],
                rows.at[k, pl.ds(j * PAIR, PAIR), pl.ds(0, GATE + WIDE)],
                dev(dy=j),
            )
            for j in range(1, NY)
        ]
        rows[k, pl.ds(0, PAIR), pl.ds(0, GATE + WIDE)] = picked[k, pl.ds(0, PAIR), :]

    def cols(k, first, size):
        return rows.at[k, :, pl.ds(first, size)]

    def side(k, j, dc=0):
        return cols(k, SIDE + (2 * j + dc) * MAIN, MAIN)

    def rows_a(k):
        for copy in to_node[k]:
            copy.wait_recv()
        row_copies[k] = [
            remote(cols(k, OWN, MAIN), side(k, 0), dev(dx=1)),
            remote(cols(k, OWN, MAIN), side(k, 1), dev(dx=-1)),
        ]
        sib_copies[k] = [remote(cols(k, OWN, WIDE), cols(k, SIB, WIDE), dev(dc=1))]

    def rows_b(k):
        for j in range(2):
            row_copies[k][j].wait_recv()
        row_copies[k].append(
            remote(
                rows.at[k, :, pl.ds(aligned(SIDE + c * 2 * MAIN), MAIN)], side(k, 2), dev(dx=toward)
            )
        )
        for j in range(2):
            sib_copies[k].append(remote(side(k, j), side(k, j, 1), dev(dc=1)))

    def rows_c(k):
        row_copies[k][2].wait_recv()
        sib_copies[k].append(remote(side(k, 2), side(k, 2, 1), dev(dc=1)))

    def hcol(k, place):
        return hid.at[k, :, pl.ds(place * WIDTH, WIDTH)]

    def up(k):
        for copy in sib_copies[k]:
            copy.wait_recv()
        gate_act = jnp.dot(rows[k, :, pl.ds(GATE, DEPTH)], wg[...], preferred_element_type=F32)
        up_act = jnp.dot(rows[k, :, pl.ds(GATE, DEPTH)], wu[...], preferred_element_type=F32)
        share = rows[k, :, pl.ds(0, GATE)].astype(F32)
        share = jnp.concatenate([share, share], axis=1)
        value = gate_act / (1.0 + jnp.exp(-gate_act)) * up_act * share
        hid[k, :, pl.ds(0, WIDTH)] = value.astype(BF16)
        hid_copies[k] = [
            remote(hcol(k, 0), hcol(k, 2), dev(dx=1)),
            remote(hcol(k, 0), hcol(k, 4), dev(dx=-1)),
        ]
        hid_sibs[k] = [remote(hcol(k, 0), hcol(k, 1), dev(dc=1))]

    def hid_b(k):
        for j in range(2):
            hid_copies[k][j].wait_recv()
        hid_copies[k].append(
            remote(
                hid.at[k, :, pl.ds(aligned((2 + 2 * c) * WIDTH), WIDTH)], hcol(k, 6), dev(dx=toward)
            )
        )
        for j in range(2):
            hid_sibs[k].append(remote(hcol(k, 2 + 2 * j), hcol(k, 3 + 2 * j), dev(dc=1)))

    def hid_c(k):
        hid_copies[k][2].wait_recv()
        hid_sibs[k].append(remote(hcol(k, 6), hcol(k, 7), dev(dc=1)))

    def down(k):
        for copy in hid_sibs[k]:
            copy.wait_recv()
        osend[k] = jnp.dot(hid[k], wd[...], preferred_element_type=F32).astype(BF16)
        to_home[k] = [
            remote(
                osend.at[k, pl.ds(j * PAIR, PAIR), :], ret.at[k, pl.ds(j * PAIR, PAIR), :], dev(dy=-j)
            )
            for j in range(1, NY)
        ]
        ret[k, pl.ds(0, PAIR), :] = osend[k, pl.ds(0, PAIR), :]

    def home(k):
        for copy in to_home[k]:
            copy.wait_recv()
        total = lax.dot_general(
            onehot[k], ret[k], (((0,), (0,)), ((), ())), preferred_element_type=F32
        )
        near, far = total[:TOK], total[TOK:]
        if k == 0:
            own[...] = near
            zso[0] = far.astype(BF16)
            z_copies[0] = [remote(zso.at[0], zsi.at[0], dev(dz=-toward))]
            return
        for copy in z_copies[k - 1]:
            copy.wait_recv()
        if k == 1:
            come = zsi[0].astype(F32)
            near = near + jnp.where(c == 0, come, 0.0)
            far = far + jnp.where(c == 1, come, 0.0)
        else:
            near = near + zsi[2 * k - 3].astype(F32)
            far = far + zsi[2 * k - 2].astype(F32)
        zso[2 * k - 1] = near.astype(BF16)
        zso[2 * k] = far.astype(BF16)
        z_copies[k] = [
            remote(zso.at[2 * k - 1], zsi.at[2 * k - 1], dev(dz=-1)),
            remote(zso.at[2 * k], zsi.at[2 * k], dev(dz=1)),
        ]

    select(1)
    arrive[4].wait_recv()
    select(0)
    select(2)
    rows_a(0)
    select(3)
    rows_b(0)
    rows_a(1)
    rows_c(0)
    for copy in weight_loads:
        copy.wait()
    up(0)
    rows_b(1)
    rows_a(2)
    hid_b(0)
    rows_c(1)
    up(1)
    hid_c(0)
    rows_b(2)
    rows_a(3)
    hid_b(1)
    down_load.wait()
    for copy in downs:
        copy.wait_recv()
    down(0)
    rows_c(2)
    up(2)
    hid_c(1)
    home(0)
    rows_b(3)
    hid_b(2)
    down(1)
    rows_c(3)
    up(3)
    hid_c(2)
    home(1)
    hid_b(3)
    down(2)
    hid_c(3)
    home(2)
    down(3)
    home(3)
    for copy in z_copies[3]:
        copy.wait_recv()
    out[...] = (own[...] + zsi[5].astype(F32) + zsi[6].astype(F32)).astype(BF16)
    for copy in remote_copies:
        copy.wait_send()


REMOTE = (3 if EARLY else 0) + 7 + 7 + 7 + 4 * (3 + 7 + 7 + 3) + 7
LOCAL = 2 + 2 * (8 + (6 if EARLY else 0))


def on_device(tokens, routes, gates, w_gate, w_up, w_down):
    any_spec = pl.BlockSpec(memory_space=pl.ANY)
    vmem_spec = pl.BlockSpec(memory_space=pltpu.VMEM)
    return pl.pallas_call(
        kernel,
        name="routed_experts",
        out_shape=jax.ShapeDtypeStruct((TOK, FEAT), BF16),
        in_specs=[any_spec, vmem_spec, vmem_spec, any_spec, any_spec, any_spec],
        out_specs=vmem_spec,
        scratch_shapes=[
            pltpu.VMEM((NZ * TOK, WIDE), BF16),
            pltpu.VMEM((NZ * 16, TOK), BF16),
            pltpu.VMEM((NZ * 16, TOK), BF16),
            pltpu.VMEM((4, ROWS, 2 * TOK), BF16),
            pltpu.VMEM((4, ROWS, GATE + WIDE), BF16),
            pltpu.VMEM((4, ROWS, GATE + DEPTH), BF16),
            pltpu.VMEM((DEPTH, WIDTH), BF16),
            pltpu.VMEM((DEPTH, WIDTH), BF16),
            pltpu.VMEM((8 * WIDTH, FEAT), BF16),
            pltpu.VMEM((4, ROWS, 8 * WIDTH), BF16),
            pltpu.VMEM((4, ROWS, FEAT), BF16),
            pltpu.VMEM((4, ROWS, FEAT), BF16),
            pltpu.VMEM((7, TOK, FEAT), BF16),
            pltpu.VMEM((7, TOK, FEAT), BF16),
            pltpu.VMEM((TOK, FEAT), F32),
            pltpu.SemaphoreType.DMA((REMOTE,)),
            pltpu.SemaphoreType.DMA((REMOTE,)),
            pltpu.SemaphoreType.DMA((LOCAL,)),
        ],
        compiler_params=pltpu.CompilerParams(
            collective_id=0, has_side_effects=True, vmem_limit_bytes=56 << 20
        ),
        cost_estimate=pl.CostEstimate(
            flops=8_500_000_000, bytes_accessed=12_000_000, transcendentals=200_000
        ),
    )(tokens, routes.T, gates.T, w_gate, w_up, w_down)


def solution(mesh):
    return jax.shard_map(
        on_device,
        mesh=mesh,
        in_specs=(
            P("node", "local"),
            P("node", None),
            P("node", None),
            P(("node", "local"), None, None),
            P(("node", "local"), None, None),
            P(("node", "local"), None, None),
        ),
        out_specs=P("node", "local"),
        check_vma=False,
    )
```

```python
import jax
import jax.numpy as jnp
from jax import lax
from jax.experimental import pallas as pl
from jax.experimental.pallas import tpu as pltpu
from jax.sharding import PartitionSpec as P

F32, BF16 = jnp.float32, jnp.bfloat16
NY, NZ, NX = 4, 8, 4
TOK = 128
FEAT = 896
WIDTH = 256
DEPTH = FEAT * 8
CAP = 24
PAIR = 2 * CAP
ROWS = NY * PAIR
HALF = ROWS // 2
EARLY = 256
MAIN = FEAT - EARLY
WIDE = MAIN + 4 * EARLY
GATE = 128
CHUNKS = ((0, 4), (3, 5), (2, 6), (1, 7))
SLOT = {0: 0, 4: 1, 3: 2, 5: 3, 2: 4, 6: 5, 1: 6, 7: 7}
OWN = GATE
SIB = GATE + WIDE
SIDE = GATE + 2 * WIDE
MISSING = -100.0
PARTS = ((0, 512), (512, 384))
EAGER = (0, 1)
ORDER = (
    "z1", "z2", "s2", "z3", "s0", "a4", "a5", "s1", "a0", "a1", "b5", "b4",
    "b0", "b1", "c5", "s3", "a3", "c0", "a2", "c1", "u0", "u1", "b3", "b2",
    "h1", "c4", "a6", "c3", "h0", "u5", "i1", "c2", "u3", "a7", "d1", "i0",
    "u2", "h3", "b6", "d0", "u4", "b7", "h5", "i3", "h2", "c6", "r0", "d3",
    "h4", "c7", "u6", "i5", "i2", "u7", "i4", "d2", "d5", "h6", "d4", "h7",
    "r1", "i6", "i7", "d6", "d7", "r2", "r3",
)


class Semaphores:
    def __init__(self, array):
        self.array, self.places, self.waited = array, {}, set()

    def at(self, name):
        return self.array.at[self.places.setdefault(name, len(self.places))]

    def wait(self, name, ref):
        if name not in self.waited:
            self.waited.add(name)
            pltpu.make_async_copy(ref, ref, self.at(name)).wait()


def kernel(
    tok, routes_t, gates_t, wg_h, wu_h, wd_h, out,
    zb, meta_out, meta_in, onehot, picked, rows, wg, wu, wd, hid, osend, ret, zso, zsi, own,
    send_sem, recv_sem, local_sem,
):
    node, local = lax.axis_index("node"), lax.axis_index("local")
    y, z, x, c = node // NZ, node % NZ, local // 2, local % 2

    def dev(dx=0, dc=0, dy=0, dz=0):
        yy, zz = (y + dy + NY) % NY, (z + dz + NZ) % NZ
        xx, cc = (x + dx + NX) % NX, (c + dc) % 2
        return (yy * NZ + zz, xx * 2 + cc)

    sent, came, loaded = Semaphores(send_sem), Semaphores(recv_sem), Semaphores(local_sem)

    def remote(src, dst, device, send, recv):
        pltpu.make_async_remote_copy(
            src_ref=src, dst_ref=dst, send_sem=sent.at(send), recv_sem=came.at(recv),
            device_id=device, device_id_type=pl.DeviceIdType.MESH,
        ).start()

    def load(src, dst, name):
        pltpu.make_async_copy(src, dst, loaded.at(name)).start()

    toward = 1 - 2 * c

    mine = zb.at[pl.ds(0, TOK), pl.ds(0, FEAT)]
    load(tok, mine, "tok")
    peers = (
        [dev(dx=i, dc=j) for i in range(NX) for j in range(2) if (i, j) != (0, 0)]
        + [dev(dy=i) for i in range(1, NY)]
        + [dev(dz=i) for i in range(1, NZ)]
    )
    barrier = pltpu.get_barrier_semaphore()
    for peer in peers:
        pl.semaphore_signal(barrier, inc=1, device_id=peer, device_id_type=pl.DeviceIdType.MESH)

    lane = lax.broadcasted_iota(jnp.int32, (TOK, TOK), 1)
    line = lax.broadcasted_iota(jnp.int32, (TOK, TOK), 0)
    step, kind = line // 16, line % 16
    target = ((y + kind % NY) % NY) * NZ + (z + step) % NZ
    expert = target * 2 + x // 2
    named = jnp.zeros((TOK, TOK), F32)
    weight = jnp.zeros((TOK, TOK), F32)
    routes_v, gates_v = routes_t[...], gates_t[...].astype(F32)
    for k in range(8):
        chosen = routes_v[k : k + 1, :]
        named = jnp.where(chosen // 2 == target, 1.0, named)
        weight = weight + jnp.where(chosen == expert, gates_v[k : k + 1, :], 0.0)
    before = jnp.where(line < lane, 1.0, 0.0).astype(BF16)
    earlier = jnp.dot(named.astype(BF16), before, preferred_element_type=F32)
    slots = jnp.where(named > 0.0, earlier, MISSING)
    meta = jnp.where(kind < 4, slots, jnp.where(kind < 8, weight, 0.0)).astype(BF16)
    meta_out[...] = meta
    meta_in[pl.ds(0, 16), :] = meta[0:16]

    loaded.wait("tok", mine)
    pl.semaphore_wait(barrier, len(peers))

    shared = zb.at[pl.ds(0, TOK), pl.ds(FEAT, 3 * EARLY)]
    for j, dx in enumerate((1, -1, 2)):
        remote(
            zb.at[pl.ds(0, TOK), pl.ds(MAIN, EARLY)],
            zb.at[pl.ds(0, TOK), pl.ds(FEAT + j * EARLY, EARLY)],
            dev(dx=dx), "first", "first",
        )

    def first_row(dx, dc):
        return (((x + dx + NX) % NX) * 2 + (c + dc) % 2) * FEAT

    def aligned(i):
        return pl.multiple_of(i, 128)

    def send_down(n):
        near = ((0, 1, 1), (1, 0, 2), (1, 1, 3), (-1, 0, 4), (-1, 1, 5))
        for dx, dc, place in (near, ((2, 0, 6), (2, 1, 7)))[n]:
            remote(
                wd_h.at[0, :, pl.ds(aligned(first_row(dx, dc)), FEAT)],
                wd.at[pl.ds(place * WIDTH, WIDTH), :],
                dev(dx=dx, dc=dc), "down", "down",
            )

    pieces = ((0, FEAT), (FEAT, 3 * EARLY))

    def part(i, p):
        return zb.at[pl.ds(SLOT[i] * TOK, TOK), pl.ds(*pieces[p])]

    def block_here(i):
        for p in range(2):
            came.wait(f"z{i}{p}", part(i, p))

    def hop(p, i):
        remote(part(i, p), part(i + 1, p), dev(dz=1), "z", f"z{i + 1}{p}")
        j = (8 - i) % 8
        remote(part(j, p), part(7 - i, p), dev(dz=-1), "z", f"z{7 - i}{p}")

    hop(0, 0)
    for n in EAGER:
        send_down(n)
    came.wait("first", shared)
    hop(1, 0)
    for i in range(1, NZ):
        remote(
            meta_out.at[pl.ds(16 * i, 16), :], meta_in.at[pl.ds(16 * SLOT[i], 16), :],
            dev(dz=i), "meta", "meta",
        )
    metas = meta_in.at[pl.ds(16, 16 * 7), :]

    def relay(i):
        for p in range(2):
            came.wait(f"z{i}{p}", part(i, p))
            came.wait(f"z{8 - i}{p}", part(8 - i, p))
            if i < 3:
                hop(p, i)
            else:
                source = zb.at[pl.ds((SLOT[3] + c) * TOK, TOK), pl.ds(*pieces[p])]
                remote(source, part(4, p), dev(dz=toward), "z", f"z4{p}")

    spans = []
    for dc in range(2):
        spans.append((first_row(0, dc), dc * WIDE, FEAT))
        for j, dx in enumerate((-1, 1, 2)):
            spans.append((first_row(dx, dc) + MAIN, dc * WIDE + FEAT + j * EARLY, EARLY))
    for j, dx in enumerate((-1, 1, 2)):
        for dc in range(2):
            spans.append((first_row(dx, dc), 2 * WIDE + (2 * j + dc) * MAIN, MAIN))
    for src, dst, size in spans:
        for name, hbm, vmem in (("wg", wg_h, wg), ("wu", wu_h, wu)):
            load(hbm.at[0, pl.ds(aligned(src), size), :], vmem.at[pl.ds(dst, size), :], name)
    own_down = wd.at[pl.ds(0, WIDTH), :]
    load(wd_h.at[0, :, pl.ds(aligned(first_row(0, 0)), FEAT)], own_down, "wd")

    def select(k):
        came.wait("meta", metas)
        for i in CHUNKS[k]:
            if i:
                block_here(i)
        near, far = (meta_in[pl.ds(16 * (2 * k + i), 16), :].astype(F32) for i in range(2))
        place = lax.broadcasted_iota(jnp.int32, (PAIR, 2 * TOK), 0).astype(F32)
        for j in range(NY):
            slot = jnp.concatenate([near[j : j + 1], far[j : j + 1] + CAP], axis=1)
            gate = jnp.concatenate([near[4 + j : 5 + j], far[4 + j : 5 + j]], axis=1)
            hit = jnp.where(place == slot, 1.0, 0.0)
            onehot[k, pl.ds(j * PAIR, PAIR), :] = hit.astype(BF16)
            share = jnp.sum(hit * gate, axis=1, keepdims=True)
            picked[k, pl.ds(j * PAIR, PAIR), pl.ds(0, GATE)] = jnp.broadcast_to(
                share, (PAIR, GATE)
            ).astype(BF16)
        chosen = jnp.dot(
            onehot[k], zb[pl.ds(2 * k * TOK, 2 * TOK), :], preferred_element_type=F32
        ).astype(BF16)
        picked[k, :, pl.ds(GATE, WIDE)] = chosen
        for j in range(1, NY):
            remote(
                picked.at[k, pl.ds(j * PAIR, PAIR), :],
                rows.at[k, pl.ds(j * PAIR, PAIR), pl.ds(0, GATE + WIDE)],
                dev(dy=j), f"y{k}", f"y{k}{j // 2}",
            )
        rows[k, pl.ds(0, PAIR), pl.ds(0, GATE + WIDE)] = picked[k, pl.ds(0, PAIR), :]

    def half(ref, q, first, size):
        return ref.at[q // 2, pl.ds(q % 2 * HALF, HALF), pl.ds(first, size)]

    def cols(q, first, size):
        return half(rows, q, first, size)

    def side(q, j, dc=0):
        return cols(q, SIDE + (2 * j + dc) * MAIN, MAIN)

    def sources(q):
        return (2, 3) if q % 2 else (1,)

    def rows_a(q):
        count = len(sources(q)) * PAIR
        place = pl.ds(sources(q)[0] * PAIR, count)
        came.wait(f"y{q // 2}{q % 2}", rows.at[q // 2, place, pl.ds(0, GATE + WIDE)])
        own_cols = cols(q, OWN, MAIN)
        remote(own_cols, side(q, 0), dev(dx=1), f"x{q}", f"x{q}")
        remote(own_cols, side(q, 1), dev(dx=-1), f"x{q}", f"x{q}")
        remote(cols(q, OWN, WIDE), cols(q, SIB, WIDE), dev(dc=1), f"x{q}", f"s{q}")

    def rows_b(q):
        came.wait(f"x{q}", cols(q, SIDE, 2 * MAIN))
        passed = cols(q, aligned(SIDE + c * 2 * MAIN), MAIN)
        remote(passed, side(q, 2), dev(dx=toward), f"x{q}", f"o{q}")
        for j in range(2):
            remote(side(q, j), side(q, j, 1), dev(dc=1), f"x{q}", f"s{q}")

    def rows_c(q):
        came.wait(f"o{q}", side(q, 2))
        remote(side(q, 2), side(q, 2, 1), dev(dc=1), f"x{q}", f"s{q}")

    def hcol(q, place):
        return half(hid, q, place * WIDTH, WIDTH)

    def up(q):
        came.wait(f"s{q}", cols(q, SIB, WIDE + 3 * MAIN))
        lines = pl.ds(q % 2 * HALF, HALF)
        given = rows[q // 2, lines, pl.ds(GATE, DEPTH)]
        gate_act = jnp.dot(given, wg[...], preferred_element_type=F32)
        up_act = jnp.dot(given, wu[...], preferred_element_type=F32)
        share = rows[q // 2, lines, pl.ds(0, GATE)].astype(F32)
        share = jnp.concatenate([share, share], axis=1)
        value = gate_act / (1.0 + jnp.exp(-gate_act)) * up_act * share
        hid[q // 2, lines, pl.ds(0, WIDTH)] = value.astype(BF16)
        remote(hcol(q, 0), hcol(q, 2), dev(dx=1), f"h{q}", f"h{q}")
        remote(hcol(q, 0), hcol(q, 4), dev(dx=-1), f"h{q}", f"h{q}")
        remote(hcol(q, 0), hcol(q, 1), dev(dc=1), f"h{q}", f"t{q}")

    def hid_b(q):
        came.wait(f"h{q}", half(hid, q, 2 * WIDTH, 2 * WIDTH))
        passed = half(hid, q, aligned((2 + 2 * c) * WIDTH), WIDTH)
        remote(passed, hcol(q, 6), dev(dx=toward), f"h{q}", f"p{q}")
        for j in range(2):
            remote(hcol(q, 2 + 2 * j), hcol(q, 3 + 2 * j), dev(dc=1), f"h{q}", f"t{q}")

    def hid_c(q):
        came.wait(f"p{q}", hcol(q, 6))
        remote(hcol(q, 6), hcol(q, 7), dev(dc=1), f"h{q}", f"t{q}")

    def down(q):
        came.wait(f"t{q}", half(hid, q, 0, 4 * WIDTH))
        loaded.wait("wd", own_down)
        came.wait("down", wd.at[pl.ds(WIDTH, 7 * WIDTH), :])
        k, lines = q // 2, pl.ds(q % 2 * HALF, HALF)
        for n, span in enumerate(PARTS):
            place = pl.ds(*span)
            osend[k, lines, place] = jnp.dot(
                hid[k, lines, :], wd[:, place], preferred_element_type=F32
            ).astype(BF16)
            for j in sources(q):
                remote(
                    osend.at[k, pl.ds(j * PAIR, PAIR), place],
                    ret.at[k, pl.ds(j * PAIR, PAIR), place],
                    dev(dy=-j), f"r{k}", f"r{k}{n}",
                )
        if q % 2 == 0:
            ret[k, pl.ds(0, PAIR), :] = osend[k, pl.ds(0, PAIR), :]

    def home(k):
        for n, span in enumerate(PARTS):
            place = pl.ds(*span)
            came.wait(f"r{k}{n}", ret.at[k, pl.ds(PAIR, 3 * PAIR), place])
            total = lax.dot_general(
                onehot[k], ret[k, :, place], (((0,), (0,)), ((), ())), preferred_element_type=F32
            )
            near, far = total[:TOK], total[TOK:]
            if k == 0:
                own[:, place] = near
                zso[0, :, place] = far.astype(BF16)
                remote(
                    zso.at[0, :, place], zsi.at[0, :, place], dev(dz=-toward), "q", f"q{k}{n}"
                )
                continue
            q = 2 * k - 1
            if k == 1:
                came.wait(f"q0{n}", zsi.at[0, :, place])
                come = zsi[0, :, place].astype(F32)
                near = near + jnp.where(c == 0, come, 0.0)
                far = far + jnp.where(c == 1, come, 0.0)
            else:
                came.wait(f"q{k - 1}{n}", zsi.at[pl.ds(q - 2, 2), :, place])
                near = near + zsi[q - 2, :, place].astype(F32)
                far = far + zsi[q - 1, :, place].astype(F32)
            zso[q, :, place] = near.astype(BF16)
            zso[q + 1, :, place] = far.astype(BF16)
            remote(zso.at[q, :, place], zsi.at[q, :, place], dev(dz=-1), "q", f"q{k}{n}")
            remote(zso.at[q + 1, :, place], zsi.at[q + 1, :, place], dev(dz=1), "q", f"q{k}{n}")

    steps = {
        "z": relay, "s": select, "a": rows_a, "b": rows_b, "c": rows_c, "u": up, "h": hid_b,
        "i": hid_c, "d": down, "r": home, "w": send_down,
    }
    for step in ORDER:
        if step[0] == "u":
            loaded.wait("wg", wg)
            loaded.wait("wu", wu)
        steps[step[0]](int(step[1]))
    for n, span in enumerate(PARTS):
        place = pl.ds(*span)
        came.wait(f"q3{n}", zsi.at[pl.ds(5, 2), :, place])
        total = own[:, place] + zsi[5, :, place].astype(F32) + zsi[6, :, place].astype(F32)
        out[:, place] = total.astype(BF16)

    sent.wait("first", shared)
    sent.wait("z", zb.at[pl.ds(TOK, 7 * TOK), :])
    sent.wait("meta", metas)
    sent.wait("down", wd.at[pl.ds(WIDTH, 7 * WIDTH), :])
    for k in range(4):
        sent.wait(f"y{k}", picked.at[k, pl.ds(PAIR, 3 * PAIR), :])
        sent.wait(f"r{k}", osend.at[k, pl.ds(PAIR, 3 * PAIR), :])
    for q in range(8):
        sent.wait(f"x{q}", cols(q, SIB, WIDE + 6 * MAIN))
        sent.wait(f"h{q}", half(hid, q, WIDTH, 7 * WIDTH))
    sent.wait("q", zso)


def on_device(tokens, routes, gates, w_gate, w_up, w_down):
    any_spec = pl.BlockSpec(memory_space=pl.ANY)
    vmem_spec = pl.BlockSpec(memory_space=pltpu.VMEM)
    return pl.pallas_call(
        kernel,
        name="routed_experts",
        out_shape=jax.ShapeDtypeStruct((TOK, FEAT), BF16),
        in_specs=[any_spec, vmem_spec, vmem_spec, any_spec, any_spec, any_spec],
        out_specs=vmem_spec,
        scratch_shapes=[
            pltpu.VMEM((NZ * TOK, WIDE), BF16),
            pltpu.VMEM((NZ * 16, TOK), BF16),
            pltpu.VMEM((NZ * 16, TOK), BF16),
            pltpu.VMEM((4, ROWS, 2 * TOK), BF16),
            pltpu.VMEM((4, ROWS, GATE + WIDE), BF16),
            pltpu.VMEM((4, ROWS, GATE + DEPTH), BF16),
            pltpu.VMEM((DEPTH, WIDTH), BF16),
            pltpu.VMEM((DEPTH, WIDTH), BF16),
            pltpu.VMEM((8 * WIDTH, FEAT), BF16),
            pltpu.VMEM((4, ROWS, 8 * WIDTH), BF16),
            pltpu.VMEM((4, ROWS, FEAT), BF16),
            pltpu.VMEM((4, ROWS, FEAT), BF16),
            pltpu.VMEM((7, TOK, FEAT), BF16),
            pltpu.VMEM((7, TOK, FEAT), BF16),
            pltpu.VMEM((TOK, FEAT), F32),
            pltpu.SemaphoreType.DMA((29,)),
            pltpu.SemaphoreType.DMA((89,)),
            pltpu.SemaphoreType.DMA((4,)),
        ],
        compiler_params=pltpu.CompilerParams(
            collective_id=0, has_side_effects=True, vmem_limit_bytes=56 << 20
        ),
        cost_estimate=pl.CostEstimate(
            flops=8_500_000_000, bytes_accessed=12_000_000, transcendentals=200_000
        ),
    )(tokens, routes.T, gates.T, w_gate, w_up, w_down)


def solution(mesh):
    return jax.shard_map(
        on_device,
        mesh=mesh,
        in_specs=(
            P("node", "local"),
            P("node", None),
            P("node", None),
            P(("node", "local"), None, None),
            P(("node", "local"), None, None),
            P(("node", "local"), None, None),
        ),
        out_specs=P("node", "local"),
        check_vma=False,
    )
```

```python
import jax
import jax.numpy as jnp
from jax import lax
from jax.experimental import pallas as pl
from jax.experimental.pallas import tpu as pltpu
from jax.sharding import PartitionSpec as P

F32, BF16 = jnp.float32, jnp.bfloat16
NY, NZ, NX = 4, 8, 4
TOK = 128
FEAT = 896
WIDTH = 256
DEPTH = FEAT * 8
CAP = 24
PAIR = 2 * CAP
ROWS = NY * PAIR
HALF = ROWS // 2
EARLY = 256
MAIN = FEAT - EARLY
WIDE = MAIN + 4 * EARLY
GATE = 128
CHUNKS = ((0, 4), (3, 5), (2, 6), (1, 7))
SLOT = {0: 0, 4: 1, 3: 2, 5: 3, 2: 4, 6: 5, 1: 6, 7: 7}
OWN = GATE
SIB = GATE + WIDE
SIDE = GATE + 2 * WIDE
MISSING = -100.0
PARTS = ((0, 384), (384, 256), (640, 256))
EAGER = (0,)
DIRECT = (6, 7)
DOWN = (
    ((0, 1, 1), (1, 0, 2), (-1, 0, 4)),
    ((1, 1, 3), (-1, 1, 5)),
    ((2, 0, 6),),
    ((2, 1, 7),),
)
ORDER = (
    "z1", "w3", "w2", "z2", "s2", "z3", "s1", "w1", "a2", "s0", "a4", "a0",
    "a3", "a1", "b0", "s3", "b3", "a5", "b1", "b2", "c0", "b4", "u0", "c3",
    "a6", "c1", "u1", "h0", "b5", "u3", "c2", "c4", "h1", "b6", "u2", "h3",
    "c5", "i1", "a7", "u4", "d1", "h2", "i0", "u5", "i3", "d0", "b7", "c6",
    "d3", "h4", "i2", "h5", "u6", "c7", "r0", "d2", "i4", "i5", "u7", "h6",
    "d5", "r1", "i6", "d4", "h7", "i7", "d6", "d7", "r2", "r3",
)


class Semaphores:
    def __init__(self, array):
        self.array, self.places, self.waited = array, {}, set()

    def at(self, name):
        return self.array.at[self.places.setdefault(name, len(self.places))]

    def wait(self, name, ref):
        if name not in self.waited:
            self.waited.add(name)
            pltpu.make_async_copy(ref, ref, self.at(name)).wait()


def kernel(
    tok, routes_t, gates_t, wg_h, wu_h, wd_h, out,
    zb, meta_out, meta_in, onehot, picked, rows, wg, wu, wd, hid, osend, ret, zso, zsi, own,
    send_sem, recv_sem, local_sem,
):
    node, local = lax.axis_index("node"), lax.axis_index("local")
    y, z = lax.div(node, NZ), lax.rem(node, NZ)
    x, c = lax.div(local, 2), lax.rem(local, 2)

    devices = {}

    def dev(dx=0, dc=0, dy=0, dz=0):
        if not isinstance(dx, int) or not isinstance(dz, int):
            return place_of(dx, dc, dy, dz)
        key = (dx % NX, dc, dy % NY, dz % NZ)
        if key not in devices:
            devices[key] = place_of(*key)
        return devices[key]

    def place_of(dx, dc, dy, dz):
        yy, zz = lax.rem(y + dy + NY, NY), lax.rem(z + dz + NZ, NZ)
        xx, cc = lax.rem(x + dx + NX, NX), lax.rem(c + dc, 2)
        return (yy * NZ + zz, xx * 2 + cc)

    sent, came, loaded = Semaphores(send_sem), Semaphores(recv_sem), Semaphores(local_sem)

    def remote(src, dst, device, send, recv):
        pltpu.make_async_remote_copy(
            src_ref=src, dst_ref=dst, send_sem=sent.at(send), recv_sem=came.at(recv),
            device_id=device, device_id_type=pl.DeviceIdType.MESH,
        ).start()

    def load(src, dst, name):
        pltpu.make_async_copy(src, dst, loaded.at(name)).start()

    toward = 1 - 2 * c

    mine = zb.at[pl.ds(0, TOK), pl.ds(0, FEAT)]
    load(tok, mine, "tok")
    peers = (
        [dev(dx=i, dc=j) for i in range(NX) for j in range(2) if (i, j) != (0, 0)]
        + [dev(dy=i) for i in range(1, NY)]
        + [dev(dz=i) for i in range(1, NZ)]
    )
    barrier = pltpu.get_barrier_semaphore()
    for peer in peers:
        pl.semaphore_signal(barrier, inc=1, device_id=peer, device_id_type=pl.DeviceIdType.MESH)

    pl.semaphore_wait(barrier, len(peers))

    shared = zb.at[pl.ds(0, TOK), pl.ds(FEAT, 3 * EARLY)]
    for j, dx in enumerate((1, -1, 2)):
        remote(
            tok.at[:, pl.ds(MAIN, EARLY)],
            zb.at[pl.ds(0, TOK), pl.ds(FEAT + j * EARLY, EARLY)],
            dev(dx=dx), "first", "first",
        )

    def first_row(dx, dc):
        return (((x + dx + NX) % NX) * 2 + (c + dc) % 2) * FEAT

    def aligned(i):
        return pl.multiple_of(i, 128)

    def send_down(n):
        for dx, dc, place in DOWN[n]:
            remote(
                wd_h.at[0, :, pl.ds(aligned(first_row(dx, dc)), FEAT)],
                wd.at[pl.ds(place * WIDTH, WIDTH), :],
                dev(dx=dx, dc=dc), "down", "down",
            )

    pieces = ((0, FEAT), (FEAT, 3 * EARLY))

    def part(i, p):
        return zb.at[pl.ds(SLOT[i] * TOK, TOK), pl.ds(*pieces[p])]

    def block_here(i):
        for p in range(2):
            came.wait(f"z{i}{p}", part(i, p))

    def hop(p, i):
        remote(part(i, p), part(i + 1, p), dev(dz=1), "z", f"z{i + 1}{p}")
        j = (8 - i) % 8
        remote(part(j, p), part(7 - i, p), dev(dz=-1), "z", f"z{7 - i}{p}")

    remote(tok, part(1, 0), dev(dz=1), "z", "z10")
    remote(tok, part(7, 0), dev(dz=-1), "z", "z70")
    for n in EAGER:
        send_down(n)
    lane = lax.broadcasted_iota(jnp.int32, (TOK, TOK), 1)
    line = lax.broadcasted_iota(jnp.int32, (TOK, TOK), 0)
    step, kind = line >> 4, line & 15
    target = ((y + kind) & (NY - 1)) * NZ + ((z + step) & (NZ - 1))
    expert = target * 2 + x // 2
    named = jnp.zeros((TOK, TOK), F32)
    weight = jnp.zeros((TOK, TOK), F32)
    routes_v, gates_v = routes_t[...], gates_t[...].astype(F32)
    for k in range(8):
        chosen = routes_v[k : k + 1, :]
        named = jnp.where(chosen >> 1 == target, 1.0, named)
        weight = weight + jnp.where(chosen == expert, gates_v[k : k + 1, :], 0.0)
    before = jnp.where(line < lane, 1.0, 0.0).astype(BF16)
    earlier = jnp.dot(named.astype(BF16), before, preferred_element_type=F32)
    slots = jnp.where(named > 0.0, earlier, MISSING)
    meta = jnp.where(kind < 4, slots, jnp.where(kind < 8, weight, 0.0)).astype(BF16)
    meta_out[...] = meta
    meta_in[pl.ds(0, 16), :] = meta[0:16]

    came.wait("first", shared)
    hop(1, 0)
    loaded.wait("tok", mine)
    for i in range(1, NZ):
        remote(
            meta_out.at[pl.ds(16 * i, 16), :], meta_in.at[pl.ds(16 * SLOT[i], 16), :],
            dev(dz=i), "meta", "meta",
        )
    metas = meta_in.at[pl.ds(16, 16 * 7), :]

    def relay(i):
        for p in range(2):
            came.wait(f"z{i}{p}", part(i, p))
            came.wait(f"z{8 - i}{p}", part(8 - i, p))
            if i < 3:
                hop(p, i)
            else:
                source = zb.at[pl.ds((SLOT[3] + c) * TOK, TOK), pl.ds(*pieces[p])]
                remote(source, part(4, p), dev(dz=toward), "z", f"z4{p}")

    spans = []
    for dc in range(2):
        spans.append((first_row(0, dc), dc * WIDE, FEAT))
        for j, dx in enumerate((-1, 1, 2)):
            spans.append((first_row(dx, dc) + MAIN, dc * WIDE + FEAT + j * EARLY, EARLY))
    for j, dx in enumerate((-1, 1, 2)):
        for dc in range(2):
            spans.append((first_row(dx, dc), 2 * WIDE + (2 * j + dc) * MAIN, MAIN))
    for src, dst, size in spans:
        for name, hbm, vmem in (("wg", wg_h, wg), ("wu", wu_h, wu)):
            load(hbm.at[0, pl.ds(aligned(src), size), :], vmem.at[pl.ds(dst, size), :], name)
    own_down = wd.at[pl.ds(0, WIDTH), :]
    load(wd_h.at[0, :, pl.ds(aligned(first_row(0, 0)), FEAT)], own_down, "wd")

    def select(k):
        came.wait("meta", metas)
        for i in CHUNKS[k]:
            if i:
                block_here(i)
        near, far = (meta_in[pl.ds(16 * (2 * k + i), 16), :].astype(F32) for i in range(2))
        place = lax.broadcasted_iota(jnp.int32, (PAIR, 2 * TOK), 0).astype(F32)
        for j in range(NY):
            slot = jnp.concatenate([near[j : j + 1], far[j : j + 1] + CAP], axis=1)
            gate = jnp.concatenate([near[4 + j : 5 + j], far[4 + j : 5 + j]], axis=1)
            hit = jnp.where(place == slot, 1.0, 0.0)
            onehot[k, pl.ds(j * PAIR, PAIR), :] = hit.astype(BF16)
            share = jnp.sum(hit * gate, axis=1, keepdims=True)
            picked[k, pl.ds(j * PAIR, PAIR), pl.ds(0, GATE)] = jnp.broadcast_to(
                share, (PAIR, GATE)
            ).astype(BF16)
        chosen = jnp.dot(
            onehot[k], zb[pl.ds(2 * k * TOK, 2 * TOK), :], preferred_element_type=F32
        ).astype(BF16)
        picked[k, :, pl.ds(GATE, WIDE)] = chosen
        for j in range(1, NY):
            remote(
                picked.at[k, pl.ds(j * PAIR, PAIR), :],
                rows.at[k, pl.ds(j * PAIR, PAIR), pl.ds(0, GATE + WIDE)],
                dev(dy=j), f"y{k}", f"y{k}{j // 2}",
            )
        rows[k, pl.ds(0, PAIR), pl.ds(0, GATE + WIDE)] = picked[k, pl.ds(0, PAIR), :]

    def half(ref, q, first, size):
        return ref.at[q // 2, pl.ds(q % 2 * HALF, HALF), pl.ds(first, size)]

    def cols(q, first, size):
        return half(rows, q, first, size)

    def side(q, j, dc=0):
        return cols(q, SIDE + (2 * j + dc) * MAIN, MAIN)

    def sources(q):
        return (2, 3) if q % 2 else (1,)

    def rows_a(q):
        count = len(sources(q)) * PAIR
        place = pl.ds(sources(q)[0] * PAIR, count)
        came.wait(f"y{q // 2}{q % 2}", rows.at[q // 2, place, pl.ds(0, GATE + WIDE)])
        own_cols = cols(q, OWN, MAIN)
        remote(own_cols, side(q, 0), dev(dx=1), f"x{q}", f"x{q}")
        remote(own_cols, side(q, 1), dev(dx=-1), f"x{q}", f"x{q}")
        remote(cols(q, OWN, WIDE), cols(q, SIB, WIDE), dev(dc=1), f"x{q}", f"s{q}")

    def rows_b(q):
        came.wait(f"x{q}", cols(q, SIDE, 2 * MAIN))
        passed = cols(q, aligned(SIDE + c * 2 * MAIN), MAIN)
        remote(passed, side(q, 2), dev(dx=toward), f"x{q}", f"o{q}")
        for j in range(2):
            remote(side(q, j), side(q, j, 1), dev(dc=1), f"x{q}", f"s{q}")

    def rows_c(q):
        came.wait(f"o{q}", side(q, 2))
        remote(side(q, 2), side(q, 2, 1), dev(dc=1), f"x{q}", f"s{q}")

    def hcol(q, place):
        return half(hid, q, place * WIDTH, WIDTH)

    def up(q):
        came.wait(f"s{q}", cols(q, SIB, WIDE + 3 * MAIN))
        lines = pl.ds(q % 2 * HALF, HALF)
        given = rows[q // 2, lines, pl.ds(GATE, DEPTH)]
        gate_act = jnp.dot(given, wg[...], preferred_element_type=F32)
        up_act = jnp.dot(given, wu[...], preferred_element_type=F32)
        share = rows[q // 2, lines, pl.ds(0, GATE)].astype(F32)
        share = jnp.concatenate([share, share], axis=1)
        value = gate_act / (1.0 + jnp.exp(-gate_act)) * up_act * share
        hid[q // 2, lines, pl.ds(0, WIDTH)] = value.astype(BF16)
        remote(hcol(q, 0), hcol(q, 2), dev(dx=1), f"h{q}", f"h{q}")
        remote(hcol(q, 0), hcol(q, 4), dev(dx=-1), f"h{q}", f"h{q}")
        if q in DIRECT:
            remote(hcol(q, 0), hcol(q, 6), dev(dx=2), f"h{q}", f"p{q}")
        remote(hcol(q, 0), hcol(q, 1), dev(dc=1), f"h{q}", f"t{q}")

    def hid_b(q):
        came.wait(f"h{q}", half(hid, q, 2 * WIDTH, 2 * WIDTH))
        if q not in DIRECT:
            passed = half(hid, q, aligned((2 + 2 * c) * WIDTH), WIDTH)
            remote(passed, hcol(q, 6), dev(dx=toward), f"h{q}", f"p{q}")
        for j in range(2):
            remote(hcol(q, 2 + 2 * j), hcol(q, 3 + 2 * j), dev(dc=1), f"h{q}", f"t{q}")

    def hid_c(q):
        came.wait(f"p{q}", hcol(q, 6))
        remote(hcol(q, 6), hcol(q, 7), dev(dc=1), f"h{q}", f"t{q}")

    def down(q):
        came.wait(f"t{q}", half(hid, q, 0, 4 * WIDTH))
        loaded.wait("wd", own_down)
        came.wait("down", wd.at[pl.ds(WIDTH, 7 * WIDTH), :])
        k, lines = q // 2, pl.ds(q % 2 * HALF, HALF)
        for n, span in enumerate(PARTS):
            place = pl.ds(*span)
            osend[k, lines, place] = jnp.dot(
                hid[k, lines, :], wd[:, place], preferred_element_type=F32
            ).astype(BF16)
            for j in sources(q):
                remote(
                    osend.at[k, pl.ds(j * PAIR, PAIR), place],
                    ret.at[k, pl.ds(j * PAIR, PAIR), place],
                    dev(dy=-j), f"r{k}", f"r{k}{n}",
                )
        if q % 2 == 0:
            ret[k, pl.ds(0, PAIR), :] = osend[k, pl.ds(0, PAIR), :]

    def home(k):
        for n, span in enumerate(PARTS):
            place = pl.ds(*span)
            came.wait(f"r{k}{n}", ret.at[k, pl.ds(PAIR, 3 * PAIR), place])
            total = lax.dot_general(
                onehot[k], ret[k, :, place], (((0,), (0,)), ((), ())), preferred_element_type=F32
            )
            near, far = total[:TOK], total[TOK:]
            if k == 0:
                own[:, place] = near
                zso[0, :, place] = far.astype(BF16)
                remote(
                    zso.at[0, :, place], zsi.at[0, :, place], dev(dz=-toward), "q", f"q{k}{n}"
                )
                continue
            q = 2 * k - 1
            if k == 1:
                came.wait(f"q0{n}", zsi.at[0, :, place])
                come = zsi[0, :, place].astype(F32)
                near = near + jnp.where(c == 0, come, 0.0)
                far = far + jnp.where(c == 1, come, 0.0)
            else:
                came.wait(f"q{k - 1}{n}", zsi.at[pl.ds(q - 2, 2), :, place])
                near = near + zsi[q - 2, :, place].astype(F32)
                far = far + zsi[q - 1, :, place].astype(F32)
            zso[q, :, place] = near.astype(BF16)
            zso[q + 1, :, place] = far.astype(BF16)
            remote(zso.at[q, :, place], zsi.at[q, :, place], dev(dz=-1), "q", f"q{k}{n}")
            remote(zso.at[q + 1, :, place], zsi.at[q + 1, :, place], dev(dz=1), "q", f"q{k}{n}")

    steps = {
        "z": relay, "s": select, "a": rows_a, "b": rows_b, "c": rows_c, "u": up, "h": hid_b,
        "i": hid_c, "d": down, "r": home, "w": send_down,
    }
    for step in ORDER:
        if step[0] == "u":
            loaded.wait("wg", wg)
            loaded.wait("wu", wu)
        steps[step[0]](int(step[1]))
    for n, span in enumerate(PARTS):
        place = pl.ds(*span)
        came.wait(f"q3{n}", zsi.at[pl.ds(5, 2), :, place])
        total = own[:, place] + zsi[5, :, place].astype(F32) + zsi[6, :, place].astype(F32)
        out[:, place] = total.astype(BF16)

    sent.wait("first", shared)
    sent.wait("z", zb.at[pl.ds(TOK, 7 * TOK), :])
    sent.wait("meta", metas)
    sent.wait("down", wd.at[pl.ds(WIDTH, 7 * WIDTH), :])
    for k in range(4):
        sent.wait(f"y{k}", picked.at[k, pl.ds(PAIR, 3 * PAIR), :])
        sent.wait(f"r{k}", osend.at[k, pl.ds(PAIR, 3 * PAIR), :])
    for q in range(8):
        sent.wait(f"x{q}", cols(q, SIB, WIDE + 6 * MAIN))
        sent.wait(f"h{q}", half(hid, q, WIDTH, 7 * WIDTH))
    sent.wait("q", zso)


def on_device(tokens, routes, gates, w_gate, w_up, w_down):
    any_spec = pl.BlockSpec(memory_space=pl.ANY)
    vmem_spec = pl.BlockSpec(memory_space=pltpu.VMEM)
    return pl.pallas_call(
        kernel,
        name="routed_experts",
        out_shape=jax.ShapeDtypeStruct((TOK, FEAT), BF16),
        in_specs=[any_spec, vmem_spec, vmem_spec, any_spec, any_spec, any_spec],
        out_specs=vmem_spec,
        scratch_shapes=[
            pltpu.VMEM((NZ * TOK, WIDE), BF16),
            pltpu.VMEM((NZ * 16, TOK), BF16),
            pltpu.VMEM((NZ * 16, TOK), BF16),
            pltpu.VMEM((4, ROWS, 2 * TOK), BF16),
            pltpu.VMEM((4, ROWS, GATE + WIDE), BF16),
            pltpu.VMEM((4, ROWS, GATE + DEPTH), BF16),
            pltpu.VMEM((DEPTH, WIDTH), BF16),
            pltpu.VMEM((DEPTH, WIDTH), BF16),
            pltpu.VMEM((8 * WIDTH, FEAT), BF16),
            pltpu.VMEM((4, ROWS, 8 * WIDTH), BF16),
            pltpu.VMEM((4, ROWS, FEAT), BF16),
            pltpu.VMEM((4, ROWS, FEAT), BF16),
            pltpu.VMEM((7, TOK, FEAT), BF16),
            pltpu.VMEM((7, TOK, FEAT), BF16),
            pltpu.VMEM((TOK, FEAT), F32),
            pltpu.SemaphoreType.DMA((29,)),
            pltpu.SemaphoreType.DMA((97,)),
            pltpu.SemaphoreType.DMA((4,)),
        ],
        compiler_params=pltpu.CompilerParams(
            collective_id=0, has_side_effects=True, vmem_limit_bytes=56 << 20
        ),
        cost_estimate=pl.CostEstimate(
            flops=8_500_000_000, bytes_accessed=12_000_000, transcendentals=200_000
        ),
    )(tokens, routes.T, gates.T, w_gate, w_up, w_down)


def solution(mesh):
    return jax.shard_map(
        on_device,
        mesh=mesh,
        in_specs=(
            P("node", "local"),
            P("node", None),
            P("node", None),
            P(("node", "local"), None, None),
            P(("node", "local"), None, None),
            P(("node", "local"), None, None),
        ),
        out_specs=P("node", "local"),
        check_vma=False,
    )
```
